256 devices in a mesh: rad: 4 (over y_hi, core), ang: 64 (over y_lo, z, x).
Axes of the slice: x: 4, y: 4 (y_hi: 2, y_lo: 2; y = y_hi * 2 + y_lo), z: 8, core: 2. Of those that a mesh axis runs over, the one named last changes fastest.
Arguments:
- adjoint_in: float32 [2, 2, 256, 256, 256], P(None, None, 'ang', 'rad'), may hold values from -6 to 6
- drift: float32 [256, 384, 768], P('rad', 'ang'), may hold values from -0.06 to 0.06
- induce: float32 [256, 384, 768], P('rad', 'ang'), may hold values from -6 to 6
- couple: float32 [256, 384, 768], P('rad', 'ang'), may hold values from -6 to 6
Outputs:
- adjoint_out: float32 [2, 2, 256, 256, 256], P(None, None, 'ang', 'rad')
The draws below stay inside these ranges and needn't reach their ends.
All inputs are finite; a program needn't handle non-finite values.
Results may differ from the reference program's by a relative error of at most 0.0003.
Values sent between devices are 32-bit elements; how exact they have to be, the bound alone decides.
A program may use at most 64 MiB of HBM per device.

```python
import math
import jax
import jax.numpy as jnp
from jax import lax

LMAX = 256
NLAT = 384
NLON = 768
RADII = 256


def level_of(stream_key, extent, pieces, smallest, high):
    factor_of, own = 1.0, jax.random.fold_in(stream_key, 6)
    for axis_at, parts in pieces:
        steps = jnp.exp(jax.random.uniform(jax.random.fold_in(own, axis_at), (parts,), jnp.float32, smallest / len(pieces), high / len(pieces)))
        factor_of = factor_of * jnp.repeat(steps, extent[axis_at] // parts).reshape([-1 if axis == axis_at else 1 for axis in range(len(extent))])
    return factor_of


def normal_values(own_key, extent, scale, most, shards=(), held_as=jnp.bfloat16):
    loudness = level_of(own_key, extent, shards, -0.22, 0.18) if shards else 1.0
    array = jax.random.normal(own_key, extent, jnp.float32) * scale * loudness
    return jnp.minimum(jnp.maximum(array, -most), most).astype(held_as)


def setup_inputs(seed: int = 0) -> dict:
    splits = jax.random.split(jax.random.key(seed), 5)
    return {
        "adjoint_in": normal_values(splits[0], (2, 2, LMAX, RADII, LMAX), 1.0, 6.0, ((2, 64), (3, 4)), jnp.float32),
        "drift": normal_values(splits[1], (RADII, NLAT, NLON), 0.01, 0.06, ((0, 4), (1, 64)), jnp.float32),
        "induce": normal_values(splits[2], (RADII, NLAT, NLON), 1.0, 6.0, ((0, 4), (1, 64)), jnp.float32),
        "couple": normal_values(splits[3], (RADII, NLAT, NLON), 1.0, 6.0, ((0, 4), (1, 64)), jnp.float32),
    }


INNER = 7.0 / 13.0
DIFFUSE = 0.5

def radial_bands():
    index = jnp.arange(RADII, dtype=jnp.float32)
    radius = INNER + 0.5 * (1.0 - jnp.cos(jnp.pi * (index + 0.5) / RADII))
    gaps = radius[1:] - radius[:-1]
    below = jnp.concatenate([gaps[:1], gaps])
    above = jnp.concatenate([gaps, gaps[-1:]])
    lower = DIFFUSE * 2.0 / ((below + above) * below)
    upper = DIFFUSE * 2.0 / ((below + above) * above)
    degree = jnp.arange(LMAX, dtype=jnp.float32)
    horizontal = DIFFUSE * degree[:, None] * (degree[:, None] + 1.0) / (radius * radius)[None, :]
    middle = 1.0 + horizontal + lower[None, :] + upper[None, :]
    zero_one = jnp.zeros((1,), jnp.float32)
    sub_band = jnp.concatenate([zero_one, -upper[:-1]])
    super_band = jnp.concatenate([-lower[1:], zero_one])
    sub_band = jnp.broadcast_to(sub_band[None, :], middle.shape)
    super_band = jnp.broadcast_to(super_band[None, :], middle.shape)
    return (sub_band, middle, super_band)

def keep_mask(orders):
    degree = jnp.arange(LMAX, dtype=jnp.int32)
    keep_degree = degree[None, :] >= orders[:, None]
    sine_ok = jnp.stack([orders >= 0, orders != 0])
    return keep_degree[None, :, None, :] & sine_ok[:, :, None, None]

def latitude_weights():
    rows = jnp.arange(NLAT, dtype=jnp.float32)
    theta = jnp.pi * (rows + 0.5) / NLAT
    return jnp.pi / NLAT * jnp.sin(theta) * 0.5

def legendre_table(orders):
    rows = jnp.arange(NLAT, dtype=jnp.float32)
    theta = jnp.pi * (rows + 0.5) / NLAT
    cosine = jnp.cos(theta)
    sine = jnp.sin(theta)
    order_f = orders.astype(jnp.float32)
    half = jnp.full_like(order_f, 0.5)
    log_start = 0.5 * jnp.log(2.0 * order_f + 1.0) + 0.5 * (lax.lgamma(order_f + 0.5) - lax.lgamma(order_f + 1.0) - lax.lgamma(half))
    start = jnp.exp(log_start[:, None] + order_f[:, None] * jnp.log(sine)[None, :])

    def advance(carry, degree):
        previous, earlier = carry
        deg_f = degree.astype(jnp.float32)
        above = degree > orders
        spread = jnp.where(above, deg_f * deg_f - order_f * order_f, 1.0)
        rise = jnp.sqrt(jnp.where(above, (4.0 * deg_f * deg_f - 1.0) / spread, 0.0))
        lower_deg = deg_f - 1.0
        damp = jnp.sqrt(jnp.maximum((lower_deg * lower_deg - order_f * order_f) / (4.0 * lower_deg * lower_deg - 1.0), 0.0))
        recur = rise[:, None] * (cosine[None, :] * previous - damp[:, None] * earlier)
        value = jnp.where(above[:, None], recur, jnp.where((degree == orders)[:, None], start, 0.0))
        return ((value, previous), value)
    zeros = jnp.zeros((orders.shape[0], NLAT), jnp.float32)
    unused, table = lax.scan(advance, (zeros, zeros), jnp.arange(LMAX, dtype=jnp.int32), unroll=16)
    return table

def trig_table():
    orders = jnp.arange(LMAX, dtype=jnp.int32)
    points = jnp.arange(NLON, dtype=jnp.int32)
    phase = orders[:, None] * points[None, :] % NLON
    angle = 2.0 * jnp.pi / NLON * phase.astype(jnp.float32)
    return jnp.stack([jnp.cos(angle), jnp.sin(angle)], axis=1)

def order_weights():
    orders = jnp.arange(LMAX, dtype=jnp.int32)
    return jnp.where(orders == 0, 1.0, 2.0).astype(jnp.float32) / NLON

def combine(harmonics, orders):
    order_f = orders.astype(jnp.float32)[:, None, None, None]
    plain = harmonics[0]
    shifted = harmonics[1]
    cos_part = plain[:, :, 0] - order_f * shifted[:, :, 1]
    sin_part = plain[:, :, 1] + order_f * shifted[:, :, 0]
    return jnp.stack([cos_part, sin_part], axis=3)

def reference(adjoint_in, drift, induce, couple):
    highest = lax.Precision.HIGHEST
    orders = jnp.arange(LMAX, dtype=jnp.int32)
    masked = jnp.where(keep_mask(orders)[None], adjoint_in, 0.0)
    sub_band, middle, super_band = radial_bands()
    stacked = masked.transpose(4, 3, 0, 1, 2)
    solved = lax.linalg.tridiagonal_solve(sub_band, middle, super_band, stacked.reshape(LMAX, RADII, -1))
    relaxed = solved.reshape(stacked.shape).transpose(2, 3, 4, 1, 0)
    table = legendre_table(orders)
    weights = latitude_weights()
    trig = trig_table()
    weighted_trig = trig * order_weights()[:, None, None]
    block_rows = math.gcd(RADII, 8)

    def per_block(start):
        relaxed_part = lax.dynamic_slice_in_dim(relaxed, start, block_rows, 3)
        fourier = jnp.einsum('lmj,fcmrl->mjfcr', table, relaxed_part, precision=highest)
        fourier = fourier * weights[None, :, None, None, None]
        grid_adjoint = jnp.einsum('mjfcr,mck->frjk', fourier, weighted_trig, precision=highest)
        drift_part = lax.dynamic_slice_in_dim(drift, start, block_rows, 0)
        induce_part = lax.dynamic_slice_in_dim(induce, start, block_rows, 0)
        couple_part = lax.dynamic_slice_in_dim(couple, start, block_rows, 0)
        plain = jnp.stack([couple_part * grid_adjoint[1], induce_part * grid_adjoint[0]])
        shifted = jnp.stack([-drift_part * grid_adjoint[0], -drift_part * grid_adjoint[1]])
        sources = jnp.stack([plain, shifted])
        harmonics = jnp.einsum('mck,sfrjk->smjcfr', trig, sources, precision=highest)
        combined = combine(harmonics, orders)
        returned = jnp.einsum('lmj,mjfcr->fcmrl', table, combined, precision=highest)
        return returned + relaxed_part
    starts = jnp.arange(0, RADII, block_rows, dtype=jnp.int32)
    blocks = lax.map(per_block, starts)
    return blocks.transpose(1, 2, 3, 0, 4, 5).reshape(2, 2, LMAX, RADII, LMAX)
```

```python
import functools

import jax
import jax.numpy as jnp
import ml_dtypes
import numpy as np
from jax import lax
from jax.experimental import pallas as pl
from jax.experimental.pallas import tpu as pltpu
from jax.sharding import PartitionSpec as P

LMAX = 256
NLAT = 384
NLON = 768
RADII = 256
RAD = 4
ANG = 64
SHELLS = RADII // RAD
INNER = 7.0 / 13.0
DIFFUSE = 0.5
F32 = jnp.float32
BF16 = jnp.bfloat16
MESH = pl.DeviceIdType.MESH


def split_np(array):
    high = array.astype(np.float32).astype(ml_dtypes.bfloat16)
    low = (array - high.astype(np.float64)).astype(np.float32).astype(ml_dtypes.bfloat16)
    return high, low


@functools.cache
def radial_constants():
    index = np.arange(RADII, dtype=np.float64)
    radius = INNER + 0.5 * (1.0 - np.cos(np.pi * (index + 0.5) / RADII))
    gaps = np.diff(radius)
    below = np.concatenate([gaps[:1], gaps])
    above = np.concatenate([gaps, gaps[-1:]])
    lower = DIFFUSE * 2.0 / ((below + above) * below)
    upper = DIFFUSE * 2.0 / ((below + above) * above)
    degree = np.arange(LMAX, dtype=np.float64)
    middle = 1.0 + DIFFUSE * (degree * (degree + 1.0))[None, :] / (radius * radius)[:, None]
    middle = middle + (lower + upper)[:, None]
    sub = np.concatenate([[0.0], -upper[:-1]])
    sup = np.concatenate([-lower[1:], [0.0]])
    inverse = np.zeros((RAD, SHELLS, LMAX))
    forward = np.zeros((RAD, SHELLS, LMAX))
    backward = np.zeros((RAD, SHELLS, LMAX))
    after = np.zeros((RAD, SHELLS, LMAX))
    before = np.zeros((RAD, SHELLS, LMAX))
    for block in range(RAD):
        base = block * SHELLS
        ratio = np.zeros((LMAX,))
        for row in range(SHELLS):
            here = sub[base + row] if row else 0.0
            inverse[block, row] = 1.0 / (middle[base + row] - here * ratio)
            forward[block, row] = -here * inverse[block, row]
            ratio = sup[base + row] * inverse[block, row]
            backward[block, row] = -ratio if row < SHELLS - 1 else 0.0

        def local_solve(right):
            swept = np.zeros((SHELLS, LMAX))
            carry = np.zeros((LMAX,))
            for row in range(SHELLS):
                carry = right[row] * inverse[block, row] + forward[block, row] * carry
                swept[row] = carry
            carry = np.zeros((LMAX,))
            for row in range(SHELLS - 1, -1, -1):
                carry = swept[row] + backward[block, row] * carry
                swept[row] = carry
            return swept

        last = np.zeros((SHELLS, LMAX))
        last[-1] = -sup[base + SHELLS - 1]
        first = np.zeros((SHELLS, LMAX))
        first[0] = -sub[base]
        after[block] = local_solve(last)
        before[block] = local_solve(first)
    coupling = np.zeros((LMAX, 2 * RAD, 2 * RAD))
    for block in range(RAD):
        for end, row in ((0, 0), (1, SHELLS - 1)):
            if block < RAD - 1:
                coupling[:, 2 * block + end, 2 * (block + 1)] = after[block, row]
            if block:
                coupling[:, 2 * block + end, 2 * (block - 1) + 1] = before[block, row]
    reduced = np.linalg.inv(np.eye(2 * RAD)[None] - coupling)
    ends = np.zeros((RAD, 2, 2 * RAD, LMAX))
    for block in range(RAD):
        if block < RAD - 1:
            ends[block, 0] = reduced[:, 2 * (block + 1), :].T
        if block:
            ends[block, 1] = reduced[:, 2 * (block - 1) + 1, :].T
    packed = np.concatenate(
        [inverse, forward, backward, after, before, ends.reshape(RAD, 4 * RAD, LMAX)], axis=1
    )
    halves = packed.reshape(RAD, 5 * SHELLS + 4 * RAD, 2, 128).transpose(0, 2, 1, 3)
    return np.ascontiguousarray(halves.astype(np.float32))


def latitude_of():
    place = np.arange(12)[:, None]
    lane = np.arange(128)[None, :] % 32
    return 6 * ((place % 2) * 32 + lane) + place // 2


@functools.cache
def legendre_constants():
    with jax.ensure_compile_time_eval(), jax.default_device(jax.devices("cpu")[0]):
        order = jnp.arange(LMAX, dtype=F32)
        log_start = 0.5 * jnp.log(2.0 * order + 1.0) + 0.5 * (
            lax.lgamma(order + 0.5) - lax.lgamma(order + 1.0) - lax.lgamma(jnp.float32(0.5))
        )
        theta = jnp.pi * (jnp.arange(NLAT, dtype=F32) + 0.5) / NLAT
        sine = np.asarray(jnp.log(jnp.sin(theta)))
        cosine = np.asarray(jnp.cos(theta))
        log_start = np.asarray(log_start)
    exponent = log_start[:, None] + (np.arange(LMAX, dtype=np.float32)[:, None] * sine[None, :])
    start = np.exp(exponent.astype(np.float32).astype(np.float64)).astype(np.float32)
    start = np.where(start < np.float32(1.1754944e-38), np.float32(0.0), start)
    rows = latitude_of()
    orders = np.arange(128) // 32
    table = np.zeros((ANG, 16, 128), np.float32)
    for block in range(ANG):
        table[block, :12] = start[4 * block + orders[None, :], rows]
    angle = np.zeros((16, 128), np.float32)
    angle[:12] = cosine[rows]
    return table, angle


@functools.cache
def weight_constants():
    rows = 6 * np.arange(ANG)[:, None] + np.arange(6)[None, :]
    theta = np.pi * (rows + 0.5) / NLAT
    weights = np.zeros((ANG, 8, 128), np.float32)
    weights[:, :6, :] = (np.pi / NLAT * np.sin(theta) * 0.5)[:, :, None]
    return weights


@functools.cache
def trig_constants():
    order = np.arange(LMAX)
    point = np.arange(NLON)
    angle = 2.0 * np.pi / NLON * ((order[:, None] * point[None, :]) % NLON)
    cosine, sine = np.cos(angle), np.sin(angle)
    weight = np.where(order == 0, 1.0, 2.0)[:, None] / NLON
    onto_grid = np.stack([cosine * weight, sine * weight], axis=1).reshape(2 * LMAX, NLON).T
    plain = np.stack([cosine, sine], axis=1).reshape(2 * LMAX, NLON)
    shifted = np.stack([-sine * order[:, None], cosine * order[:, None]], axis=1)
    shifted = shifted.reshape(2 * LMAX, NLON)
    onto_grid = onto_grid.reshape(3, 256, 2 * LMAX)
    back = np.stack([plain.reshape(512, 3, 256), shifted.reshape(512, 3, 256)], axis=2)
    back = back.transpose(1, 0, 2, 3).reshape(3, 512, 512)
    return split_np(onto_grid) + split_np(back)


def split(value):
    high = value.astype(BF16)
    return high, (value - high.astype(F32)).astype(BF16)


NN = (((1,), (0,)), ((), ()))
NT = (((1,), (1,)), ((), ()))


def product(left, right, dims):
    dot = functools.partial(lax.dot_general, dimension_numbers=dims, preferred_element_type=F32)
    return dot(left[0], right[0]) + (dot(left[0], right[1]) + dot(left[1], right[0]))


def kernel(
    adj_hbm, drift_hbm, induce_hbm, couple_hbm, tri_hbm, start_hbm, weight_hbm, angle_ref,
    wh_hbm, wl_hbm, ah_hbm, al_hbm,
    out_ref,
    adj, rel, tri, start, weight, tb, rise_ref, damp_ref, tth, ttl, rbh, rbl,
    ends, xs, xr, cs, yr, drift, induce, couple, mp, md, wh, wl, ah, al, acc,
    in_sem, ends_send, ends_recv, xs_sem, xr_sem, cs_sem, yr_sem,
):
    rho = lax.axis_index("rad")
    me = lax.axis_index("ang")
    y, z, x = me // 32, lax.rem(me // 4, 8), lax.rem(me, 4)

    def peer(step):
        other = lax.rem(step * 37, 64)
        py = lax.rem(y + other // 32, 2)
        pz = lax.rem(z + lax.rem(other // 4, 8), 8)
        px = lax.rem(x + lax.rem(other, 4), 4)
        return py * 32 + pz * 4 + px

    def rad_peer(step):
        return lax.rem(rho + step, RAD)

    loads = [
        pltpu.make_async_copy(adj_hbm.at[:, pl.ds(0, 128)], adj.at[0], in_sem.at[0]),
        pltpu.make_async_copy(adj_hbm.at[:, pl.ds(128, 128)], adj.at[1], in_sem.at[1]),
        pltpu.make_async_copy(tri_hbm.at[rho], tri, in_sem.at[2]),
        pltpu.make_async_copy(start_hbm.at[me], start, in_sem.at[3]),
        pltpu.make_async_copy(weight_hbm.at[me], weight, in_sem.at[4]),
        pltpu.make_async_copy(wh_hbm, wh, in_sem.at[5]),
        pltpu.make_async_copy(wl_hbm, wl, in_sem.at[6]),
        pltpu.make_async_copy(ah_hbm, ah, in_sem.at[7]),
        pltpu.make_async_copy(al_hbm, al, in_sem.at[8]),
        pltpu.make_async_copy(drift_hbm, drift, in_sem.at[9]),
        pltpu.make_async_copy(induce_hbm, induce, in_sem.at[10]),
        pltpu.make_async_copy(couple_hbm, couple, in_sem.at[11]),
    ]
    for load in loads:
        load.start()

    barrier = pltpu.get_barrier_semaphore()

    def greet(step, unused):
        pl.semaphore_signal(barrier, inc=1, device_id=(rho, peer(step)), device_id_type=MESH)
        return unused

    for step in range(1, RAD):
        pl.semaphore_signal(barrier, inc=1, device_id=(rad_peer(step), me), device_id_type=MESH)
    lax.fori_loop(1, ANG, greet, 0)

    lane_order = 4 * me + lax.broadcasted_iota(jnp.int32, (32, 128), 1) // 32
    order_f = lane_order.astype(F32)

    def factors(block, unused):
        degree = block * 32 + lax.broadcasted_iota(jnp.int32, (32, 128), 0)
        deg_f = degree.astype(F32)
        above = degree > lane_order
        spread = jnp.where(above, deg_f * deg_f - order_f * order_f, 1.0)
        square = jnp.where(above, (4.0 * deg_f * deg_f - 1.0) / spread, 1.0)
        rise_ref[pl.ds(block * 32, 32), :] = jnp.where(above, jnp.sqrt(square), 0.0)
        low = deg_f - 1.0
        square = jnp.maximum((low * low - order_f * order_f) / (4.0 * low * low - 1.0), 0.0)
        damp_ref[pl.ds(block * 32, 32), :] = jnp.sqrt(square)
        return unused

    lax.fori_loop(0, 8, factors, 0)

    for load in loads[:3]:
        load.wait()
    row_id = lax.broadcasted_iota(jnp.int32, (16, 128), 0)
    row_order = 4 * me + lax.rem(row_id, 4)
    sine_zero = jnp.logical_and(row_order == 0, lax.rem(row_id // 4, 2) == 1)
    lanes = lax.broadcasted_iota(jnp.int32, (16, 128), 1)
    keeps = [
        jnp.logical_and(lanes + 128 * half >= row_order, jnp.logical_not(sine_zero))
        for half in range(2)
    ]

    def tri_row(row, half):
        return tri[half, pl.ds(row, 1), :]

    def sweep(row, carry):
        result = []
        for half in range(2):
            right = adj[half, pl.ds(row, 16, stride=64), :]
            right = jnp.where(keeps[half], right, 0.0) * tri_row(row, half)
            value = right + tri_row(SHELLS + row, half) * carry[half]
            rel[half, pl.ds(row, 16, stride=64), :] = value
            result.append(value)
        return tuple(result)

    zero = jnp.zeros((16, 128), F32)
    blank = jnp.where(keeps[0], 0.0, zero)
    lax.fori_loop(0, SHELLS, sweep, (blank, blank), unroll=4)

    def unsweep(step, carry):
        row = SHELLS - 1 - step
        result = []
        for half in range(2):
            value = rel[half, pl.ds(row, 16, stride=64), :]
            value = value + tri_row(2 * SHELLS + row, half) * carry[half]
            rel[half, pl.ds(row, 16, stride=64), :] = value
            result.append(value)
        return tuple(result)

    lax.fori_loop(0, SHELLS, unsweep, (blank, blank), unroll=4)
    for half in range(2):
        for end, row in ((0, 0), (1, SHELLS - 1)):
            ends[rho, pl.ds(16 * end, 16), 128 * half : 128 * half + 128] = rel[
                half, pl.ds(row, 16, stride=64), :
            ]

    pl.semaphore_wait(barrier, ANG - 1 + RAD - 1)
    for step in range(1, RAD):
        pltpu.make_async_remote_copy(
            src_ref=ends.at[rho],
            dst_ref=ends.at[rho],
            send_sem=ends_send,
            recv_sem=ends_recv,
            device_id=(rad_peer(step), me),
            device_id_type=MESH,
        ).start()

    loads[3].wait()
    cosine = angle_ref[...]
    begin = start[...]
    nothing = begin * 0.0
    wide_order = 4 * me + lax.broadcasted_iota(jnp.int32, (16, 128), 1) // 32

    def advance(degree, carry):
        previous, earlier = carry
        rise = rise_ref[pl.ds(degree, 1), :]
        damp = damp_ref[pl.ds(degree, 1), :]
        value = rise * (cosine * previous - damp * earlier)
        value = jnp.where(wide_order == degree, begin, value)
        tb[pl.ds(pl.multiple_of(degree * 16, 16), 16), :] = value
        return value, previous

    lax.fori_loop(0, LMAX, advance, (nothing, nothing), unroll=8)

    for place in range(12):
        turned = tb[pl.ds(place, LMAX, stride=16), :].T
        high, low = split(turned)
        for order in range(4):
            tth[order, 32 * place : 32 * place + 32, :] = high[32 * order : 32 * order + 32]
            ttl[order, 32 * place : 32 * place + 32, :] = low[32 * order : 32 * order + 32]

    block_ends = ends.at[pl.ds(0, RAD - 1)]
    pltpu.make_async_copy(block_ends, block_ends, ends_recv).wait()
    outer = []
    for half in range(2):
        cols = slice(128 * half, 128 * half + 128)
        pair = []
        for side in range(2):
            total = zero
            for source in range(RAD):
                for end in range(2):
                    factor = tri_row(5 * SHELLS + 8 * side + 2 * source + end, half)
                    total = total + factor * ends[source, 16 * end : 16 * end + 16, cols]
            pair.append(total)
        outer.append(pair)

    def correct(row, unused):
        for half in range(2):
            value = rel[half, pl.ds(row, 16, stride=64), :]
            value = value + tri_row(3 * SHELLS + row, half) * outer[half][0]
            value = value + tri_row(4 * SHELLS + row, half) * outer[half][1]
            rel[half, pl.ds(row, 16, stride=64), :] = value
        return unused

    lax.fori_loop(0, SHELLS, correct, 0, unroll=4)

    for order in range(4):
        for part in range(2):
            for field in range(2):
                rows = pl.ds(((2 * field + part) * 4 + order) * 64, 64)
                value = jnp.concatenate([rel[0, rows, :], rel[1, rows, :]], axis=1)
                high, low = split(value)
                at = (2 * part + field) * 64
                rbh[order, at : at + 64, :] = high
                rbl[order, at : at + 64, :] = low
                acc[order, at : at + 64, :] = value

    def send_part(part, source, target, send_sem, recv_sem):
        def send(step, unused):
            other = peer(step)
            pltpu.make_async_remote_copy(
                src_ref=source.at[pl.ds(2 * part, 2), pl.ds(pl.multiple_of(other * 8, 8), 8), :],
                dst_ref=target.at[pl.ds(2 * part, 2), pl.ds(pl.multiple_of(me * 8, 8), 8), :],
                send_sem=send_sem.at[part],
                recv_sem=recv_sem.at[part],
                device_id=(rho, other),
                device_id_type=MESH,
            ).start()
            return unused

        lax.fori_loop(1, ANG, send, 0)
        own = pl.ds(pl.multiple_of(me * 8, 8), 8)
        for t in range(2 * part, 2 * part + 2):
            target[t, own, :] = source[t, own, :]

    def wait_part(part, target, sem):
        block = target.at[pl.ds(2 * part, 2), pl.ds(0, (ANG - 1) * 8), :]
        pltpu.make_async_copy(block, block, sem.at[part]).wait()

    for part in range(3):
        rows = slice(128 * part, 128 * part + 128)
        for order in range(4):
            value = product(
                (tth[order, rows, :], ttl[order, rows, :]), (rbh[order], rbl[order]), NT
            )
            for trig in range(2):
                for t in range(2):
                    xs[2 * part + t, pl.ds(2 * order + trig, 64, stride=8), :] = value[
                        64 * t : 64 * t + 64, 128 * trig : 128 * trig + 128
                    ]
        send_part(part, xs, xr, xs_sem, xr_sem)

    for load in loads[4:]:
        load.wait()
    for t in range(6):
        for block in range(6):
            cols = slice(128 * block, 128 * block + 128)
            scale = weight[t : t + 1, :]
            pair = jnp.concatenate([couple[:, t, cols], induce[:, t, cols]], axis=0)
            mp[t, cols, :] = pair.T * scale
            turn = drift[:, t, cols]
            md[t, cols, :] = jnp.concatenate([turn, turn], axis=0).T * (-scale)

    for part in range(3):
        wait_part(part, xr, xr_sem)
        first, second = 2 * part, 2 * part + 1
        field = split(jnp.concatenate([xr[first], xr[second]], axis=1))

        acc_c = jnp.zeros((512, 256), F32)
        for block in range(3):
            grid = product((wh[block], wl[block]), field, NN)
            rows = slice(256 * block, 256 * block + 256)
            sides = []
            for t in range(2):
                here = grid[:, 128 * t : 128 * t + 128]
                plain = mp[2 * part + t, rows, :] * pltpu.roll(here, 64, 1)
                sides.append(jnp.concatenate([plain, md[2 * part + t, rows, :] * here], axis=0))
            source = split(jnp.concatenate(sides, axis=1))
            acc_c = acc_c + product((ah[block], al[block]), source, NN)
        cs[first] = acc_c[:, :128]
        cs[second] = acc_c[:, 128:]
        send_part(part, cs, yr, cs_sem, yr_sem)

    for part in range(3):
        wait_part(part, yr, yr_sem)
        rows = slice(128 * part, 128 * part + 128)
        for order in range(4):
            sides = []
            for trig in range(2):
                pair = [yr[2 * part + t, pl.ds(2 * order + trig, 64, stride=8), :] for t in range(2)]
                sides.append(jnp.concatenate(pair, axis=0).T)
            value = split(jnp.concatenate(sides, axis=0))
            acc[order] = acc[order] + product(value, (tth[order, rows, :], ttl[order, rows, :]), NN)

    for order in range(4):
        for trig in range(2):
            for field in range(2):
                at = ((2 * field + trig) * 4 + order) * 64
                here = (2 * trig + field) * 64
                out_ref[at : at + 64, :] = acc[order, here : here + 64, :]

    pltpu.make_async_copy(block_ends, block_ends, ends_send).wait()
    for part in range(3):
        wait_part(part, xs, xs_sem)
        wait_part(part, cs, cs_sem)


def per_device(adjoint_in, drift, induce, couple):
    wh, wl, ah, al = trig_constants()
    start, angle = legendre_constants()
    anywhere = pl.BlockSpec(memory_space=pl.ANY)
    vmem = pl.BlockSpec(memory_space=pltpu.VMEM)
    result = pl.pallas_call(
        kernel,
        out_shape=jax.ShapeDtypeStruct((1024, LMAX), F32),
        in_specs=[anywhere] * 7 + [vmem] + [anywhere] * 4,
        out_specs=vmem,
        scratch_shapes=[
            pltpu.VMEM((2, 1024, 128), F32),
            pltpu.VMEM((2, 1024, 128), F32),
            pltpu.VMEM((2, 336, 128), F32),
            pltpu.VMEM((16, 128), F32),
            pltpu.VMEM((8, 128), F32),
            pltpu.VMEM((LMAX * 16, 128), F32),
            pltpu.VMEM((LMAX, 128), F32),
            pltpu.VMEM((LMAX, 128), F32),
            pltpu.VMEM((4, NLAT, LMAX), BF16),
            pltpu.VMEM((4, NLAT, LMAX), BF16),
            pltpu.VMEM((4, 256, LMAX), BF16),
            pltpu.VMEM((4, 256, LMAX), BF16),
            pltpu.VMEM((RAD, 32, LMAX), F32),
            pltpu.VMEM((6, 512, 128), F32),
            pltpu.VMEM((6, 512, 128), F32),
            pltpu.VMEM((6, 512, 128), F32),
            pltpu.VMEM((6, 512, 128), F32),
            pltpu.VMEM((SHELLS, 6, NLON), F32),
            pltpu.VMEM((SHELLS, 6, NLON), F32),
            pltpu.VMEM((SHELLS, 6, NLON), F32),
            pltpu.VMEM((6, NLON, 128), F32),
            pltpu.VMEM((6, NLON, 128), F32),
            pltpu.VMEM((3, 256, 512), BF16),
            pltpu.VMEM((3, 256, 512), BF16),
            pltpu.VMEM((3, 512, 512), BF16),
            pltpu.VMEM((3, 512, 512), BF16),
            pltpu.VMEM((4, 256, LMAX), F32),
            pltpu.SemaphoreType.DMA((12,)),
            pltpu.SemaphoreType.DMA,
            pltpu.SemaphoreType.DMA,
            pltpu.SemaphoreType.DMA((3,)),
            pltpu.SemaphoreType.DMA((3,)),
            pltpu.SemaphoreType.DMA((3,)),
            pltpu.SemaphoreType.DMA((3,)),
        ],
        compiler_params=pltpu.CompilerParams(
            collective_id=0, has_side_effects=True, vmem_limit_bytes=56 * 1024 * 1024
        ),
    )(
        adjoint_in.reshape(1024, LMAX), drift, induce, couple,
        jnp.asarray(radial_constants()), jnp.asarray(start), jnp.asarray(weight_constants()),
        jnp.asarray(angle), jnp.asarray(wh), jnp.asarray(wl), jnp.asarray(ah), jnp.asarray(al),
    )
    return result.reshape(2, 2, 4, SHELLS, LMAX)


def solution(mesh):
    return jax.shard_map(
        per_device,
        mesh=mesh,
        in_specs=(
            P(None, None, "ang", "rad", None),
            P("rad", "ang", None),
            P("rad", "ang", None),
            P("rad", "ang", None),
        ),
        out_specs=P(None, None, "ang", "rad", None),
        check_vma=False,
    )
```

```python
import functools

import jax
import jax.numpy as jnp
import ml_dtypes
import numpy as np
from jax import lax
from jax.experimental import pallas as pl
from jax.experimental.pallas import tpu as pltpu
from jax.sharding import PartitionSpec as P

LMAX = 256
NLAT = 384
NLON = 768
RADII = 256
RAD = 4
ANG = 64
SHELLS = RADII // RAD
INNER = 7.0 / 13.0
DIFFUSE = 0.5
F32 = jnp.float32
BF16 = jnp.bfloat16
MESH = pl.DeviceIdType.MESH


def split_np(array):
    high = array.astype(np.float32).astype(ml_dtypes.bfloat16)
    low = (array - high.astype(np.float64)).astype(np.float32).astype(ml_dtypes.bfloat16)
    return high, low


@functools.cache
def radial_constants():
    index = np.arange(RADII, dtype=np.float64)
    radius = INNER + 0.5 * (1.0 - np.cos(np.pi * (index + 0.5) / RADII))
    gaps = np.diff(radius)
    below = np.concatenate([gaps[:1], gaps])
    above = np.concatenate([gaps, gaps[-1:]])
    lower = DIFFUSE * 2.0 / ((below + above) * below)
    upper = DIFFUSE * 2.0 / ((below + above) * above)
    degree = np.arange(LMAX, dtype=np.float64)
    middle = 1.0 + DIFFUSE * (degree * (degree + 1.0))[None, :] / (radius * radius)[:, None]
    middle = middle + (lower + upper)[:, None]
    sub = np.concatenate([[0.0], -upper[:-1]])
    sup = np.concatenate([-lower[1:], [0.0]])
    inverse = np.zeros((RAD, SHELLS, LMAX))
    forward = np.zeros((RAD, SHELLS, LMAX))
    backward = np.zeros((RAD, SHELLS, LMAX))
    after = np.zeros((RAD, SHELLS, LMAX))
    before = np.zeros((RAD, SHELLS, LMAX))
    for block in range(RAD):
        base = block * SHELLS
        ratio = np.zeros((LMAX,))
        for row in range(SHELLS):
            here = sub[base + row] if row else 0.0
            inverse[block, row] = 1.0 / (middle[base + row] - here * ratio)
            forward[block, row] = -here * inverse[block, row]
            ratio = sup[base + row] * inverse[block, row]
            backward[block, row] = -ratio if row < SHELLS - 1 else 0.0

        def local_solve(right):
            swept = np.zeros((SHELLS, LMAX))
            carry = np.zeros((LMAX,))
            for row in range(SHELLS):
                carry = right[row] * inverse[block, row] + forward[block, row] * carry
                swept[row] = carry
            carry = np.zeros((LMAX,))
            for row in range(SHELLS - 1, -1, -1):
                carry = swept[row] + backward[block, row] * carry
                swept[row] = carry
            return swept

        last = np.zeros((SHELLS, LMAX))
        last[-1] = -sup[base + SHELLS - 1]
        first = np.zeros((SHELLS, LMAX))
        first[0] = -sub[base]
        after[block] = local_solve(last)
        before[block] = local_solve(first)
    coupling = np.zeros((LMAX, 2 * RAD, 2 * RAD))
    for block in range(RAD):
        for end, row in ((0, 0), (1, SHELLS - 1)):
            if block < RAD - 1:
                coupling[:, 2 * block + end, 2 * (block + 1)] = after[block, row]
            if block:
                coupling[:, 2 * block + end, 2 * (block - 1) + 1] = before[block, row]
    reduced = np.linalg.inv(np.eye(2 * RAD)[None] - coupling)
    ends = np.zeros((RAD, 2, 2 * RAD, LMAX))
    for block in range(RAD):
        if block < RAD - 1:
            ends[block, 0] = reduced[:, 2 * (block + 1), :].T
        if block:
            ends[block, 1] = reduced[:, 2 * (block - 1) + 1, :].T
    packed = np.concatenate(
        [inverse, forward, backward, after, before, ends.reshape(RAD, 4 * RAD, LMAX)], axis=1
    )
    halves = packed.reshape(RAD, 5 * SHELLS + 4 * RAD, 2, 128).transpose(0, 2, 1, 3)
    return np.ascontiguousarray(halves.astype(np.float32))


def latitude_of():
    place = np.arange(12)[:, None]
    lane = np.arange(128)[None, :] % 32
    return 6 * ((place % 2) * 32 + lane) + place // 2


@functools.cache
def legendre_constants():
    with jax.ensure_compile_time_eval(), jax.default_device(jax.devices("cpu")[0]):
        order = jnp.arange(LMAX, dtype=F32)
        log_start = 0.5 * jnp.log(2.0 * order + 1.0) + 0.5 * (
            lax.lgamma(order + 0.5) - lax.lgamma(order + 1.0) - lax.lgamma(jnp.float32(0.5))
        )
        theta = jnp.pi * (jnp.arange(NLAT, dtype=F32) + 0.5) / NLAT
        sine = np.asarray(jnp.log(jnp.sin(theta)))
        cosine = np.asarray(jnp.cos(theta))
        log_start = np.asarray(log_start)
    exponent = log_start[:, None] + (np.arange(LMAX, dtype=np.float32)[:, None] * sine[None, :])
    start = np.exp(exponent.astype(np.float32).astype(np.float64)).astype(np.float32)
    start = np.where(start < np.float32(1.1754944e-38), np.float32(0.0), start)
    rows = latitude_of()
    orders = np.arange(128) // 32
    table = np.zeros((ANG, 16, 128), np.float32)
    for block in range(ANG):
        table[block, :12] = start[4 * block + orders[None, :], rows]
    angle = np.zeros((16, 128), np.float32)
    angle[:12] = cosine[rows]
    return table, angle


@functools.cache
def weight_constants():
    rows = 6 * np.arange(ANG)[:, None] + np.arange(6)[None, :]
    theta = np.pi * (rows + 0.5) / NLAT
    weights = np.zeros((ANG, 8, 128), np.float32)
    weights[:, :6, :] = (np.pi / NLAT * np.sin(theta) * 0.5)[:, :, None]
    return weights


@functools.cache
def trig_constants():
    order = np.arange(LMAX)
    point = np.arange(NLON)
    angle = 2.0 * np.pi / NLON * ((order[:, None] * point[None, :]) % NLON)
    cosine, sine = np.cos(angle), np.sin(angle)
    weight = np.where(order == 0, 1.0, 2.0)[:, None] / NLON
    onto_grid = np.stack([cosine * weight, sine * weight], axis=1).reshape(2 * LMAX, NLON).T
    plain = np.stack([cosine, sine], axis=1).reshape(2 * LMAX, NLON)
    shifted = np.stack([-sine * order[:, None], cosine * order[:, None]], axis=1)
    shifted = shifted.reshape(2 * LMAX, NLON)
    onto_grid = onto_grid.reshape(3, 256, 2 * LMAX)
    back = np.stack([plain.reshape(512, 3, 256), shifted.reshape(512, 3, 256)], axis=2)
    back = back.transpose(1, 0, 2, 3).reshape(3, 512, 512)
    return split_np(onto_grid) + split_np(back)


def split(value):
    high = value.astype(BF16)
    return high, (value - high.astype(F32)).astype(BF16)


NN = (((1,), (0,)), ((), ()))
NT = (((1,), (1,)), ((), ()))


def product(left, right, dims):
    dot = functools.partial(lax.dot_general, dimension_numbers=dims, preferred_element_type=F32)
    return dot(left[0], right[0]) + (dot(left[0], right[1]) + dot(left[1], right[0]))


def kernel(
    adj_hbm, drift_hbm, induce_hbm, couple_hbm, tri_hbm, start_hbm, weight_hbm, angle_ref,
    wh_hbm, wl_hbm, ah_hbm, al_hbm,
    out_ref,
    adj, rel, tri, start, weight, tb, rise_ref, damp_ref, tth, ttl, rbh, rbl,
    ends, xs, xr, cs, yr, drift, induce, couple, mp, md, wh, wl, ah, al, acc,
    in_sem, out_sem, ends_send, ends_recv, xs_sem, xr_sem, cs_sem, yr_sem,
):
    rho = lax.axis_index("rad")
    me = lax.axis_index("ang")
    y, z, x = me // 32, lax.rem(me // 4, 8), lax.rem(me, 4)

    def peer(step):
        other = lax.rem(step * 37, 64)
        py = lax.rem(y + other // 32, 2)
        pz = lax.rem(z + lax.rem(other // 4, 8), 8)
        px = lax.rem(x + lax.rem(other, 4), 4)
        return py * 32 + pz * 4 + px

    def rad_peer(step):
        return lax.rem(rho + step, RAD)

    loads = [
        pltpu.make_async_copy(adj_hbm.at[:, pl.ds(0, 128)], adj.at[0], in_sem.at[0]),
        pltpu.make_async_copy(adj_hbm.at[:, pl.ds(128, 128)], adj.at[1], in_sem.at[1]),
        pltpu.make_async_copy(tri_hbm.at[rho], tri, in_sem.at[2]),
        pltpu.make_async_copy(start_hbm.at[me], start, in_sem.at[3]),
        pltpu.make_async_copy(weight_hbm.at[me], weight, in_sem.at[4]),
        pltpu.make_async_copy(wh_hbm, wh, in_sem.at[5]),
        pltpu.make_async_copy(wl_hbm, wl, in_sem.at[6]),
        pltpu.make_async_copy(ah_hbm, ah, in_sem.at[7]),
        pltpu.make_async_copy(al_hbm, al, in_sem.at[8]),
        pltpu.make_async_copy(drift_hbm, drift, in_sem.at[9]),
        pltpu.make_async_copy(induce_hbm, induce, in_sem.at[10]),
        pltpu.make_async_copy(couple_hbm, couple, in_sem.at[11]),
    ]
    for load in loads:
        load.start()

    barrier = pltpu.get_barrier_semaphore()

    def greet(step, unused):
        pl.semaphore_signal(barrier, inc=1, device_id=(rho, peer(step)), device_id_type=MESH)
        return unused

    for step in range(1, RAD):
        pl.semaphore_signal(barrier, inc=1, device_id=(rad_peer(step), me), device_id_type=MESH)
    lax.fori_loop(1, ANG, greet, 0)

    lane_order = 4 * me + lax.broadcasted_iota(jnp.int32, (32, 128), 1) // 32
    order_f = lane_order.astype(F32)

    def factors(block, unused):
        degree = block * 32 + lax.broadcasted_iota(jnp.int32, (32, 128), 0)
        deg_f = degree.astype(F32)
        above = degree > lane_order
        spread = jnp.where(above, deg_f * deg_f - order_f * order_f, 1.0)
        square = jnp.where(above, (4.0 * deg_f * deg_f - 1.0) / spread, 1.0)
        rise_ref[pl.ds(block * 32, 32), :] = jnp.where(above, jnp.sqrt(square), 0.0)
        low = deg_f - 1.0
        square = jnp.maximum((low * low - order_f * order_f) / (4.0 * low * low - 1.0), 0.0)
        damp_ref[pl.ds(block * 32, 32), :] = jnp.sqrt(square)
        return unused

    lax.fori_loop(0, 8, factors, 0)

    for load in loads[:3]:
        load.wait()
    row_id = lax.broadcasted_iota(jnp.int32, (16, 128), 0)
    row_order = 4 * me + lax.rem(row_id, 4)
    sine_zero = jnp.logical_and(row_order == 0, lax.rem(row_id // 4, 2) == 1)
    lanes = lax.broadcasted_iota(jnp.int32, (16, 128), 1)
    keeps = [
        jnp.logical_and(lanes + 128 * half >= row_order, jnp.logical_not(sine_zero))
        for half in range(2)
    ]

    def tri_row(row, half):
        return tri[half, pl.ds(row, 1), :]

    def sweep(row, carry):
        result = []
        for half in range(2):
            right = adj[half, pl.ds(row, 16, stride=64), :]
            right = jnp.where(keeps[half], right, 0.0) * tri_row(row, half)
            value = right + tri_row(SHELLS + row, half) * carry[half]
            rel[half, pl.ds(row, 16, stride=64), :] = value
            result.append(value)
        return tuple(result)

    zero = jnp.zeros((16, 128), F32)
    blank = jnp.where(keeps[0], 0.0, zero)
    lax.fori_loop(0, SHELLS, sweep, (blank, blank), unroll=4)

    def unsweep(step, carry):
        row = SHELLS - 1 - step
        result = []
        for half in range(2):
            value = rel[half, pl.ds(row, 16, stride=64), :]
            value = value + tri_row(2 * SHELLS + row, half) * carry[half]
            rel[half, pl.ds(row, 16, stride=64), :] = value
            result.append(value)
        return tuple(result)

    lax.fori_loop(0, SHELLS, unsweep, (blank, blank), unroll=4)
    for half in range(2):
        for end, row in ((0, 0), (1, SHELLS - 1)):
            ends[rho, pl.ds(16 * end, 16), 128 * half : 128 * half + 128] = rel[
                half, pl.ds(row, 16, stride=64), :
            ]

    pl.semaphore_wait(barrier, ANG - 1 + RAD - 1)
    for step in range(1, RAD):
        pltpu.make_async_remote_copy(
            src_ref=ends.at[rho],
            dst_ref=ends.at[rho],
            send_sem=ends_send,
            recv_sem=ends_recv,
            device_id=(rad_peer(step), me),
            device_id_type=MESH,
        ).start()

    loads[3].wait()
    cosine = angle_ref[...]
    begin = start[...]
    nothing = begin * 0.0
    wide_order = 4 * me + lax.broadcasted_iota(jnp.int32, (16, 128), 1) // 32

    def advance(degree, carry):
        previous, earlier = carry
        rise = rise_ref[pl.ds(degree, 1), :]
        damp = damp_ref[pl.ds(degree, 1), :]
        value = rise * (cosine * previous - damp * earlier)
        value = jnp.where(wide_order == degree, begin, value)
        tb[pl.ds(pl.multiple_of(degree * 16, 16), 16), :] = value
        return value, previous

    lax.fori_loop(0, LMAX, advance, (nothing, nothing), unroll=8)

    for place in range(12):
        turned = tb[pl.ds(place, LMAX, stride=16), :].T
        high, low = split(turned)
        for order in range(4):
            tth[order, 32 * place : 32 * place + 32, :] = high[32 * order : 32 * order + 32]
            ttl[order, 32 * place : 32 * place + 32, :] = low[32 * order : 32 * order + 32]

    block_ends = ends.at[pl.ds(0, RAD - 1)]
    pltpu.make_async_copy(block_ends, block_ends, ends_recv).wait()
    outer = []
    for half in range(2):
        cols = slice(128 * half, 128 * half + 128)
        pair = []
        for side in range(2):
            total = zero
            for source in range(RAD):
                for end in range(2):
                    factor = tri_row(5 * SHELLS + 8 * side + 2 * source + end, half)
                    total = total + factor * ends[source, 16 * end : 16 * end + 16, cols]
            pair.append(total)
        outer.append(pair)

    def correct(row, unused):
        for half in range(2):
            value = rel[half, pl.ds(row, 16, stride=64), :]
            value = value + tri_row(3 * SHELLS + row, half) * outer[half][0]
            value = value + tri_row(4 * SHELLS + row, half) * outer[half][1]
            rel[half, pl.ds(row, 16, stride=64), :] = value
        return unused

    lax.fori_loop(0, SHELLS, correct, 0, unroll=4)

    for order in range(4):
        for part in range(2):
            for field in range(2):
                rows = pl.ds(((2 * field + part) * 4 + order) * 64, 64)
                value = jnp.concatenate([rel[0, rows, :], rel[1, rows, :]], axis=1)
                high, low = split(value)
                at = (2 * part + field) * 64
                rbh[order, at : at + 64, :] = high
                rbl[order, at : at + 64, :] = low
                acc[rows, :] = value

    def send_part(part, source, target, send_sem, recv_sem):
        def send(step, unused):
            other = peer(step)
            pltpu.make_async_remote_copy(
                src_ref=source.at[pl.ds(2 * part, 2), pl.ds(pl.multiple_of(other * 8, 8), 8), :],
                dst_ref=target.at[pl.ds(2 * part, 2), pl.ds(pl.multiple_of(me * 8, 8), 8), :],
                send_sem=send_sem.at[part],
                recv_sem=recv_sem.at[part],
                device_id=(rho, other),
                device_id_type=MESH,
            ).start()
            return unused

        lax.fori_loop(1, ANG, send, 0)
        own = pl.ds(pl.multiple_of(me * 8, 8), 8)
        for t in range(2 * part, 2 * part + 2):
            target[t, own, :] = source[t, own, :]

    def wait_part(part, target, sem):
        block = target.at[pl.ds(2 * part, 2), pl.ds(0, (ANG - 1) * 8), :]
        pltpu.make_async_copy(block, block, sem.at[part]).wait()

    for part in range(3):
        rows = slice(128 * part, 128 * part + 128)
        for order in range(4):
            value = product(
                (tth[order, rows, :], ttl[order, rows, :]), (rbh[order], rbl[order]), NT
            )
            for trig in range(2):
                for t in range(2):
                    xs[2 * part + t, pl.ds(2 * order + trig, 64, stride=8), :] = value[
                        64 * t : 64 * t + 64, 128 * trig : 128 * trig + 128
                    ]
        send_part(part, xs, xr, xs_sem, xr_sem)

    for load in loads[4:]:
        load.wait()
    for t in range(6):
        for block in range(6):
            cols = slice(128 * block, 128 * block + 128)
            scale = weight[t : t + 1, :]
            pair = jnp.concatenate([couple[t, :, cols], induce[t, :, cols]], axis=0)
            mp[t, cols, :] = pair.T * scale
            turn = drift[t, :, cols]
            md[t, cols, :] = jnp.concatenate([turn, turn], axis=0).T * (-scale)

    for part in range(3):
        wait_part(part, xr, xr_sem)
        first, second = 2 * part, 2 * part + 1
        field = split(jnp.concatenate([xr[first], xr[second]], axis=1))

        acc_c = jnp.zeros((512, 256), F32)
        for block in range(3):
            grid = product((wh[block], wl[block]), field, NN)
            rows = slice(256 * block, 256 * block + 256)
            sides = []
            for t in range(2):
                here = grid[:, 128 * t : 128 * t + 128]
                plain = mp[2 * part + t, rows, :] * pltpu.roll(here, 64, 1)
                sides.append(jnp.concatenate([plain, md[2 * part + t, rows, :] * here], axis=0))
            source = split(jnp.concatenate(sides, axis=1))
            acc_c = acc_c + product((ah[block], al[block]), source, NN)
        cs[first] = acc_c[:, :128]
        cs[second] = acc_c[:, 128:]
        send_part(part, cs, yr, cs_sem, yr_sem)

    stores = []
    for part in range(3):
        wait_part(part, yr, yr_sem)
        rows = slice(128 * part, 128 * part + 128)
        for order in range(4):
            sides = []
            for trig in range(2):
                pair = [yr[2 * part + t, pl.ds(2 * order + trig, 64, stride=8), :] for t in range(2)]
                sides.append(jnp.concatenate(pair, axis=0).T)
            value = split(jnp.concatenate(sides, axis=0))
            value = product(value, (tth[order, rows, :], ttl[order, rows, :]), NN)
            for trig in range(2):
                for field in range(2):
                    at = ((2 * field + trig) * 4 + order) * 64
                    here = (2 * trig + field) * 64
                    acc[at : at + 64, :] = acc[at : at + 64, :] + value[here : here + 64, :]
                    if part == 2:
                        result_rows = pl.ds(at, 64)
                        stores.append(
                            pltpu.make_async_copy(
                                acc.at[result_rows], out_ref.at[result_rows], out_sem.at[len(stores)]
                            )
                        )
                        stores[-1].start()

    pltpu.make_async_copy(block_ends, block_ends, ends_send).wait()
    for part in range(3):
        wait_part(part, xs, xs_sem)
        wait_part(part, cs, cs_sem)
    for store in stores:
        store.wait()


def per_device(adjoint_in, drift, induce, couple):
    wh, wl, ah, al = trig_constants()
    start, angle = legendre_constants()
    anywhere = pl.BlockSpec(memory_space=pl.ANY)
    vmem = pl.BlockSpec(memory_space=pltpu.VMEM)
    result = pl.pallas_call(
        kernel,
        out_shape=jax.ShapeDtypeStruct((1024, LMAX), F32),
        in_specs=[anywhere] * 7 + [vmem] + [anywhere] * 4,
        out_specs=anywhere,
        scratch_shapes=[
            pltpu.VMEM((2, 1024, 128), F32),
            pltpu.VMEM((2, 1024, 128), F32),
            pltpu.VMEM((2, 336, 128), F32),
            pltpu.VMEM((16, 128), F32),
            pltpu.VMEM((8, 128), F32),
            pltpu.VMEM((LMAX * 16, 128), F32),
            pltpu.VMEM((LMAX, 128), F32),
            pltpu.VMEM((LMAX, 128), F32),
            pltpu.VMEM((4, NLAT, LMAX), BF16),
            pltpu.VMEM((4, NLAT, LMAX), BF16),
            pltpu.VMEM((4, 256, LMAX), BF16),
            pltpu.VMEM((4, 256, LMAX), BF16),
            pltpu.VMEM((RAD, 32, LMAX), F32),
            pltpu.VMEM((6, 512, 128), F32),
            pltpu.VMEM((6, 512, 128), F32),
            pltpu.VMEM((6, 512, 128), F32),
            pltpu.VMEM((6, 512, 128), F32),
            pltpu.VMEM((6, SHELLS, NLON), F32),
            pltpu.VMEM((6, SHELLS, NLON), F32),
            pltpu.VMEM((6, SHELLS, NLON), F32),
            pltpu.VMEM((6, NLON, 128), F32),
            pltpu.VMEM((6, NLON, 128), F32),
            pltpu.VMEM((3, 256, 512), BF16),
            pltpu.VMEM((3, 256, 512), BF16),
            pltpu.VMEM((3, 512, 512), BF16),
            pltpu.VMEM((3, 512, 512), BF16),
            pltpu.VMEM((1024, LMAX), F32),
            pltpu.SemaphoreType.DMA((12,)),
            pltpu.SemaphoreType.DMA((16,)),
            pltpu.SemaphoreType.DMA,
            pltpu.SemaphoreType.DMA,
            pltpu.SemaphoreType.DMA((3,)),
            pltpu.SemaphoreType.DMA((3,)),
            pltpu.SemaphoreType.DMA((3,)),
            pltpu.SemaphoreType.DMA((3,)),
        ],
        compiler_params=pltpu.CompilerParams(
            collective_id=0, has_side_effects=True, vmem_limit_bytes=56 * 1024 * 1024
        ),
    )(
        adjoint_in.reshape(1024, LMAX),
        drift.transpose(1, 0, 2), induce.transpose(1, 0, 2), couple.transpose(1, 0, 2),
        jnp.asarray(radial_constants()), jnp.asarray(start), jnp.asarray(weight_constants()),
        jnp.asarray(angle), jnp.asarray(wh), jnp.asarray(wl), jnp.asarray(ah), jnp.asarray(al),
    )
    return result.reshape(2, 2, 4, SHELLS, LMAX)


def solution(mesh):
    return jax.shard_map(
        per_device,
        mesh=mesh,
        in_specs=(
            P(None, None, "ang", "rad", None),
            P("rad", "ang", None),
            P("rad", "ang", None),
            P("rad", "ang", None),
        ),
        out_specs=P(None, None, "ang", "rad", None),
        check_vma=False,
    )
```

```python
import functools

import jax
import jax.numpy as jnp
import ml_dtypes
import numpy as np
from jax import lax
from jax.experimental import pallas as pl
from jax.experimental.pallas import tpu as pltpu
from jax.sharding import PartitionSpec as P

LMAX = 256
NLAT = 384
NLON = 768
RADII = 256
RAD = 4
ANG = 64
SHELLS = RADII // RAD
INNER = 7.0 / 13.0
DIFFUSE = 0.5
F32 = jnp.float32
BF16 = jnp.bfloat16
MESH = pl.DeviceIdType.MESH


def split_np(array):
    high = array.astype(np.float32).astype(ml_dtypes.bfloat16)
    low = (array - high.astype(np.float64)).astype(np.float32).astype(ml_dtypes.bfloat16)
    return high, low


@functools.cache
def radial_constants():
    index = np.arange(RADII, dtype=np.float64)
    radius = INNER + 0.5 * (1.0 - np.cos(np.pi * (index + 0.5) / RADII))
    gaps = np.diff(radius)
    below = np.concatenate([gaps[:1], gaps])
    above = np.concatenate([gaps, gaps[-1:]])
    lower = DIFFUSE * 2.0 / ((below + above) * below)
    upper = DIFFUSE * 2.0 / ((below + above) * above)
    degree = np.arange(LMAX, dtype=np.float64)
    middle = 1.0 + DIFFUSE * (degree * (degree + 1.0))[None, :] / (radius * radius)[:, None]
    middle = middle + (lower + upper)[:, None]
    sub = np.concatenate([[0.0], -upper[:-1]])
    sup = np.concatenate([-lower[1:], [0.0]])
    inverse = np.zeros((RAD, SHELLS, LMAX))
    forward = np.zeros((RAD, SHELLS, LMAX))
    backward = np.zeros((RAD, SHELLS, LMAX))
    after = np.zeros((RAD, SHELLS, LMAX))
    before = np.zeros((RAD, SHELLS, LMAX))
    for block in range(RAD):
        base = block * SHELLS
        ratio = np.zeros((LMAX,))
        for row in range(SHELLS):
            here = sub[base + row] if row else 0.0
            inverse[block, row] = 1.0 / (middle[base + row] - here * ratio)
            forward[block, row] = -here * inverse[block, row]
            ratio = sup[base + row] * inverse[block, row]
            backward[block, row] = -ratio if row < SHELLS - 1 else 0.0

        def local_solve(right):
            swept = np.zeros((SHELLS, LMAX))
            carry = np.zeros((LMAX,))
            for row in range(SHELLS):
                carry = right[row] * inverse[block, row] + forward[block, row] * carry
                swept[row] = carry
            carry = np.zeros((LMAX,))
            for row in range(SHELLS - 1, -1, -1):
                carry = swept[row] + backward[block, row] * carry
                swept[row] = carry
            return swept

        last = np.zeros((SHELLS, LMAX))
        last[-1] = -sup[base + SHELLS - 1]
        first = np.zeros((SHELLS, LMAX))
        first[0] = -sub[base]
        after[block] = local_solve(last)
        before[block] = local_solve(first)
    coupling = np.zeros((LMAX, 2 * RAD, 2 * RAD))
    for block in range(RAD):
        for end, row in ((0, 0), (1, SHELLS - 1)):
            if block < RAD - 1:
                coupling[:, 2 * block + end, 2 * (block + 1)] = after[block, row]
            if block:
                coupling[:, 2 * block + end, 2 * (block - 1) + 1] = before[block, row]
    reduced = np.linalg.inv(np.eye(2 * RAD)[None] - coupling)
    ends = np.zeros((RAD, 2, 2 * RAD, LMAX))
    for block in range(RAD):
        if block < RAD - 1:
            ends[block, 0] = reduced[:, 2 * (block + 1), :].T
        if block:
            ends[block, 1] = reduced[:, 2 * (block - 1) + 1, :].T
    packed = np.concatenate(
        [inverse, forward, backward, after, before, ends.reshape(RAD, 4 * RAD, LMAX)], axis=1
    )
    halves = packed.reshape(RAD, 5 * SHELLS + 4 * RAD, 2, 128).transpose(0, 2, 1, 3)
    return np.ascontiguousarray(halves.astype(np.float32))


def latitude_of():
    place = np.arange(12)[:, None]
    lane = np.arange(128)[None, :] % 32
    return 6 * ((place % 2) * 32 + lane) + place // 2


@functools.cache
def legendre_constants():
    with jax.ensure_compile_time_eval(), jax.default_device(jax.devices("cpu")[0]):
        order = jnp.arange(LMAX, dtype=F32)
        log_start = 0.5 * jnp.log(2.0 * order + 1.0) + 0.5 * (
            lax.lgamma(order + 0.5) - lax.lgamma(order + 1.0) - lax.lgamma(jnp.float32(0.5))
        )
        theta = jnp.pi * (jnp.arange(NLAT, dtype=F32) + 0.5) / NLAT
        sine = np.asarray(jnp.log(jnp.sin(theta)))
        cosine = np.asarray(jnp.cos(theta))
        log_start = np.asarray(log_start)
    exponent = log_start[:, None] + (np.arange(LMAX, dtype=np.float32)[:, None] * sine[None, :])
    start = np.exp(exponent.astype(np.float32).astype(np.float64)).astype(np.float32)
    start = np.where(start < np.float32(1.1754944e-38), np.float32(0.0), start)
    rows = latitude_of()
    orders = np.arange(128) // 32
    table = np.zeros((ANG, 16, 128), np.float32)
    for block in range(ANG):
        table[block, :12] = start[4 * block + orders[None, :], rows]
    angle = np.zeros((16, 128), np.float32)
    angle[:12] = cosine[rows]
    return table, angle


@functools.cache
def weight_constants():
    rows = 6 * np.arange(ANG)[:, None] + np.arange(6)[None, :]
    theta = np.pi * (rows + 0.5) / NLAT
    weights = np.zeros((ANG, 8, 128), np.float32)
    weights[:, :6, :] = (np.pi / NLAT * np.sin(theta) * 0.5)[:, :, None]
    return weights


@functools.cache
def trig_constants():
    order = np.arange(LMAX)
    point = np.arange(NLON)
    angle = 2.0 * np.pi / NLON * ((order[:, None] * point[None, :]) % NLON)
    cosine, sine = np.cos(angle), np.sin(angle)
    weight = np.where(order == 0, 1.0, 2.0)[:, None] / NLON
    onto_grid = np.stack([cosine * weight, sine * weight], axis=1).reshape(2 * LMAX, NLON).T
    plain = np.stack([cosine, sine], axis=1).reshape(2 * LMAX, NLON)
    shifted = np.stack([-sine * order[:, None], cosine * order[:, None]], axis=1)
    shifted = shifted.reshape(2 * LMAX, NLON)
    onto_grid = onto_grid.reshape(3, 256, 2 * LMAX)
    back = np.stack([plain.reshape(512, 3, 256), shifted.reshape(512, 3, 256)], axis=2)
    back = back.transpose(1, 0, 2, 3).reshape(3, 512, 512)
    return split_np(onto_grid) + split_np(back)


def split(value):
    high = value.astype(BF16)
    return high, (value - high.astype(F32)).astype(BF16)


NN = (((1,), (0,)), ((), ()))
NT = (((1,), (1,)), ((), ()))


def product(left, right, dims):
    dot = functools.partial(lax.dot_general, dimension_numbers=dims, preferred_element_type=F32)
    return dot(left[0], right[0]) + (dot(left[0], right[1]) + dot(left[1], right[0]))


def kernel(
    adj_hbm, drift_hbm, induce_hbm, couple_hbm, tri_hbm, start_hbm, weight_hbm, angle_ref,
    wh_hbm, wl_hbm, ah_hbm, al_hbm,
    out_ref,
    adj, rel, tri, start, weight, tb, rise_ref, damp_ref, tth, ttl, rbh, rbl,
    ends, xs, xr, cs, yr, drift, induce, couple, mp, md, wh, wl, ah, al, acc,
    in_sem, out_sem, ends_send, ends_recv, xs_sem, xr_sem, cs_sem, yr_sem,
):
    rho = lax.axis_index("rad")
    me = lax.axis_index("ang")
    y, z, x = me // 32, lax.rem(me // 4, 8), lax.rem(me, 4)

    def peer(step):
        other = lax.rem(step * 37, 64)
        py = lax.rem(y + other // 32, 2)
        pz = lax.rem(z + lax.rem(other // 4, 8), 8)
        px = lax.rem(x + lax.rem(other, 4), 4)
        return py * 32 + pz * 4 + px

    def rad_peer(step):
        return lax.rem(rho + step, RAD)

    loads = [
        pltpu.make_async_copy(adj_hbm.at[:, pl.ds(0, 128)], adj.at[0], in_sem.at[0]),
        pltpu.make_async_copy(adj_hbm.at[:, pl.ds(128, 128)], adj.at[1], in_sem.at[1]),
        pltpu.make_async_copy(tri_hbm.at[rho], tri, in_sem.at[2]),
        pltpu.make_async_copy(start_hbm.at[me], start, in_sem.at[3]),
        pltpu.make_async_copy(weight_hbm.at[me], weight, in_sem.at[4]),
        pltpu.make_async_copy(wh_hbm, wh, in_sem.at[5]),
        pltpu.make_async_copy(wl_hbm, wl, in_sem.at[6]),
        pltpu.make_async_copy(ah_hbm, ah, in_sem.at[7]),
        pltpu.make_async_copy(al_hbm, al, in_sem.at[8]),
        pltpu.make_async_copy(drift_hbm, drift, in_sem.at[9]),
        pltpu.make_async_copy(induce_hbm, induce, in_sem.at[10]),
        pltpu.make_async_copy(couple_hbm, couple, in_sem.at[11]),
    ]
    for load in loads:
        load.start()

    barrier = pltpu.get_barrier_semaphore()

    def greet(step, unused):
        pl.semaphore_signal(barrier, inc=1, device_id=(rho, peer(step)), device_id_type=MESH)
        return unused

    for step in range(1, RAD):
        pl.semaphore_signal(barrier, inc=1, device_id=(rad_peer(step), me), device_id_type=MESH)
    lax.fori_loop(1, ANG, greet, 0)

    for load in loads[:3]:
        load.wait()
    row_id = lax.broadcasted_iota(jnp.int32, (16, 128), 0)
    row_order = 4 * me + lax.rem(row_id, 4)
    sine_zero = jnp.logical_and(row_order == 0, lax.rem(row_id // 4, 2) == 1)
    lanes = lax.broadcasted_iota(jnp.int32, (16, 128), 1)
    keeps = [
        jnp.logical_and(lanes + 128 * half >= row_order, jnp.logical_not(sine_zero))
        for half in range(2)
    ]

    def tri_row(row, half):
        return tri[half, pl.ds(row, 1), :]

    def sweep(row, carry):
        result = []
        for half in range(2):
            right = adj[half, pl.ds(row, 16, stride=64), :]
            right = jnp.where(keeps[half], right, 0.0) * tri_row(row, half)
            value = right + tri_row(SHELLS + row, half) * carry[half]
            rel[half, pl.ds(row, 16, stride=64), :] = value
            result.append(value)
        return tuple(result)

    zero = jnp.zeros((16, 128), F32)
    blank = jnp.where(keeps[0], 0.0, zero)
    lax.fori_loop(0, SHELLS, sweep, (blank, blank), unroll=8)

    def unsweep(step, carry):
        row = SHELLS - 1 - step
        result = []
        for half in range(2):
            value = rel[half, pl.ds(row, 16, stride=64), :]
            value = value + tri_row(2 * SHELLS + row, half) * carry[half]
            rel[half, pl.ds(row, 16, stride=64), :] = value
            result.append(value)
        return tuple(result)

    lax.fori_loop(0, SHELLS, unsweep, (blank, blank), unroll=8)
    for half in range(2):
        for end, row in ((0, 0), (1, SHELLS - 1)):
            ends[rho, pl.ds(16 * end, 16), 128 * half : 128 * half + 128] = rel[
                half, pl.ds(row, 16, stride=64), :
            ]

    pl.semaphore_wait(barrier, ANG - 1 + RAD - 1)
    for step in range(1, RAD):
        pltpu.make_async_remote_copy(
            src_ref=ends.at[rho],
            dst_ref=ends.at[rho],
            send_sem=ends_send,
            recv_sem=ends_recv,
            device_id=(rad_peer(step), me),
            device_id_type=MESH,
        ).start()

    lane_order = 4 * me + lax.broadcasted_iota(jnp.int32, (32, 128), 1) // 32
    order_f = lane_order.astype(F32)

    def factors(block, unused):
        degree = block * 32 + lax.broadcasted_iota(jnp.int32, (32, 128), 0)
        deg_f = degree.astype(F32)
        above = degree > lane_order
        spread = jnp.where(above, deg_f * deg_f - order_f * order_f, 1.0)
        square = jnp.where(above, (4.0 * deg_f * deg_f - 1.0) / spread, 1.0)
        rise_ref[pl.ds(block * 32, 32), :] = jnp.where(above, jnp.sqrt(square), 0.0)
        low = deg_f - 1.0
        square = jnp.maximum((low * low - order_f * order_f) / (4.0 * low * low - 1.0), 0.0)
        damp_ref[pl.ds(block * 32, 32), :] = jnp.sqrt(square)
        return unused

    lax.fori_loop(0, 8, factors, 0)

    loads[3].wait()
    cosine = angle_ref[...]
    begin = start[...]
    nothing = begin * 0.0
    wide_order = 4 * me + lax.broadcasted_iota(jnp.int32, (16, 128), 1) // 32

    def advance(degree, carry):
        previous, earlier = carry
        rise = rise_ref[pl.ds(degree, 1), :]
        damp = damp_ref[pl.ds(degree, 1), :]
        value = rise * (cosine * previous - damp * earlier)
        value = jnp.where(wide_order == degree, begin, value)
        tb[pl.ds(pl.multiple_of(degree * 16, 16), 16), :] = value
        return value, previous

    lax.fori_loop(0, LMAX, advance, (nothing, nothing), unroll=8)

    for place in range(12):
        turned = tb[pl.ds(place, LMAX, stride=16), :].T
        high, low = split(turned)
        for order in range(4):
            tth[order, 32 * place : 32 * place + 32, :] = high[32 * order : 32 * order + 32]
            ttl[order, 32 * place : 32 * place + 32, :] = low[32 * order : 32 * order + 32]

    block_ends = ends.at[pl.ds(0, RAD - 1)]
    pltpu.make_async_copy(block_ends, block_ends, ends_recv).wait()
    outer = []
    for half in range(2):
        cols = slice(128 * half, 128 * half + 128)
        pair = []
        for side in range(2):
            total = zero
            for source in range(RAD):
                for end in range(2):
                    factor = tri_row(5 * SHELLS + 8 * side + 2 * source + end, half)
                    total = total + factor * ends[source, 16 * end : 16 * end + 16, cols]
            pair.append(total)
        outer.append(pair)

    def correct(row, unused):
        for half in range(2):
            value = rel[half, pl.ds(row, 16, stride=64), :]
            value = value + tri_row(3 * SHELLS + row, half) * outer[half][0]
            value = value + tri_row(4 * SHELLS + row, half) * outer[half][1]
            rel[half, pl.ds(row, 16, stride=64), :] = value
        return unused

    lax.fori_loop(0, SHELLS, correct, 0, unroll=4)

    for order in range(4):
        for part in range(2):
            for field in range(2):
                rows = pl.ds(((2 * field + part) * 4 + order) * 64, 64)
                value = jnp.concatenate([rel[0, rows, :], rel[1, rows, :]], axis=1)
                high, low = split(value)
                at = (2 * part + field) * 64
                rbh[order, at : at + 64, :] = high
                rbl[order, at : at + 64, :] = low
                acc[rows, :] = value

    def send_part(part, source, target, send_sem, recv_sem):
        def send(step, unused):
            other = peer(step)
            pltpu.make_async_remote_copy(
                src_ref=source.at[pl.ds(2 * part, 2), pl.ds(pl.multiple_of(other * 8, 8), 8), :],
                dst_ref=target.at[pl.ds(2 * part, 2), pl.ds(pl.multiple_of(me * 8, 8), 8), :],
                send_sem=send_sem.at[part],
                recv_sem=recv_sem.at[part],
                device_id=(rho, other),
                device_id_type=MESH,
            ).start()
            return unused

        lax.fori_loop(1, ANG, send, 0)
        own = pl.ds(pl.multiple_of(me * 8, 8), 8)
        for t in range(2 * part, 2 * part + 2):
            target[t, own, :] = source[t, own, :]

    def wait_part(part, target, sem):
        block = target.at[pl.ds(2 * part, 2), pl.ds(0, (ANG - 1) * 8), :]
        pltpu.make_async_copy(block, block, sem.at[part]).wait()

    for part in range(3):
        rows = slice(128 * part, 128 * part + 128)
        for order in range(4):
            value = product(
                (tth[order, rows, :], ttl[order, rows, :]), (rbh[order], rbl[order]), NT
            )
            for trig in range(2):
                for t in range(2):
                    xs[2 * part + t, pl.ds(2 * order + trig, 64, stride=8), :] = value[
                        64 * t : 64 * t + 64, 128 * trig : 128 * trig + 128
                    ]
        send_part(part, xs, xr, xs_sem, xr_sem)

    for load in loads[4:]:
        load.wait()
    for t in range(6):
        for block in range(6):
            cols = slice(128 * block, 128 * block + 128)
            scale = weight[t : t + 1, :]
            pair = jnp.concatenate([couple[t, :, cols], induce[t, :, cols]], axis=0)
            mp[t, cols, :] = pair.T * scale
            turn = drift[t, :, cols]
            md[t, cols, :] = jnp.concatenate([turn, turn], axis=0).T * (-scale)

    for part in range(3):
        wait_part(part, xr, xr_sem)
        first, second = 2 * part, 2 * part + 1
        field = split(jnp.concatenate([xr[first], xr[second]], axis=1))

        acc_c = jnp.zeros((512, 256), F32)
        for block in range(3):
            grid = product((wh[block], wl[block]), field, NN)
            rows = slice(256 * block, 256 * block + 256)
            sides = []
            for t in range(2):
                here = grid[:, 128 * t : 128 * t + 128]
                plain = mp[2 * part + t, rows, :] * pltpu.roll(here, 64, 1)
                sides.append(jnp.concatenate([plain, md[2 * part + t, rows, :] * here], axis=0))
            source = split(jnp.concatenate(sides, axis=1))
            acc_c = acc_c + product((ah[block], al[block]), source, NN)
        cs[first] = acc_c[:, :128]
        cs[second] = acc_c[:, 128:]
        send_part(part, cs, yr, cs_sem, yr_sem)

    stores = []
    for part in range(3):
        wait_part(part, yr, yr_sem)
        rows = slice(128 * part, 128 * part + 128)
        for order in range(4):
            sides = []
            for trig in range(2):
                pair = [yr[2 * part + t, pl.ds(2 * order + trig, 64, stride=8), :] for t in range(2)]
                sides.append(jnp.concatenate(pair, axis=0).T)
            value = split(jnp.concatenate(sides, axis=0))
            value = product(value, (tth[order, rows, :], ttl[order, rows, :]), NN)
            for trig in range(2):
                for field in range(2):
                    at = ((2 * field + trig) * 4 + order) * 64
                    here = (2 * trig + field) * 64
                    acc[at : at + 64, :] = acc[at : at + 64, :] + value[here : here + 64, :]
                    if part == 2:
                        result_rows = pl.ds(at, 64)
                        stores.append(
                            pltpu.make_async_copy(
                                acc.at[result_rows], out_ref.at[result_rows], out_sem.at[len(stores)]
                            )
                        )
                        stores[-1].start()

    pltpu.make_async_copy(block_ends, block_ends, ends_send).wait()
    for part in range(3):
        wait_part(part, xs, xs_sem)
        wait_part(part, cs, cs_sem)
    for store in stores:
        store.wait()


def per_device(adjoint_in, drift, induce, couple):
    wh, wl, ah, al = trig_constants()
    start, angle = legendre_constants()
    anywhere = pl.BlockSpec(memory_space=pl.ANY)
    vmem = pl.BlockSpec(memory_space=pltpu.VMEM)
    result = pl.pallas_call(
        kernel,
        out_shape=jax.ShapeDtypeStruct((1024, LMAX), F32),
        in_specs=[anywhere] * 7 + [vmem] + [anywhere] * 4,
        out_specs=anywhere,
        scratch_shapes=[
            pltpu.VMEM((2, 1024, 128), F32),
            pltpu.VMEM((2, 1024, 128), F32),
            pltpu.VMEM((2, 336, 128), F32),
            pltpu.VMEM((16, 128), F32),
            pltpu.VMEM((8, 128), F32),
            pltpu.VMEM((LMAX * 16, 128), F32),
            pltpu.VMEM((LMAX, 128), F32),
            pltpu.VMEM((LMAX, 128), F32),
            pltpu.VMEM((4, NLAT, LMAX), BF16),
            pltpu.VMEM((4, NLAT, LMAX), BF16),
            pltpu.VMEM((4, 256, LMAX), BF16),
            pltpu.VMEM((4, 256, LMAX), BF16),
            pltpu.VMEM((RAD, 32, LMAX), F32),
            pltpu.VMEM((6, 512, 128), F32),
            pltpu.VMEM((6, 512, 128), F32),
            pltpu.VMEM((6, 512, 128), F32),
            pltpu.VMEM((6, 512, 128), F32),
            pltpu.VMEM((6, SHELLS, NLON), F32),
            pltpu.VMEM((6, SHELLS, NLON), F32),
            pltpu.VMEM((6, SHELLS, NLON), F32),
            pltpu.VMEM((6, NLON, 128), F32),
            pltpu.VMEM((6, NLON, 128), F32),
            pltpu.VMEM((3, 256, 512), BF16),
            pltpu.VMEM((3, 256, 512), BF16),
            pltpu.VMEM((3, 512, 512), BF16),
            pltpu.VMEM((3, 512, 512), BF16),
            pltpu.VMEM((1024, LMAX), F32),
            pltpu.SemaphoreType.DMA((12,)),
            pltpu.SemaphoreType.DMA((16,)),
            pltpu.SemaphoreType.DMA,
            pltpu.SemaphoreType.DMA,
            pltpu.SemaphoreType.DMA((3,)),
            pltpu.SemaphoreType.DMA((3,)),
            pltpu.SemaphoreType.DMA((3,)),
            pltpu.SemaphoreType.DMA((3,)),
        ],
        compiler_params=pltpu.CompilerParams(
            collective_id=0, has_side_effects=True, vmem_limit_bytes=56 * 1024 * 1024
        ),
    )(
        adjoint_in.reshape(1024, LMAX),
        drift.transpose(1, 0, 2), induce.transpose(1, 0, 2), couple.transpose(1, 0, 2),
        jnp.asarray(radial_constants()), jnp.asarray(start), jnp.asarray(weight_constants()),
        jnp.asarray(angle), jnp.asarray(wh), jnp.asarray(wl), jnp.asarray(ah), jnp.asarray(al),
    )
    return result.reshape(2, 2, 4, SHELLS, LMAX)


def solution(mesh):
    return jax.shard_map(
        per_device,
        mesh=mesh,
        in_specs=(
            P(None, None, "ang", "rad", None),
            P("rad", "ang", None),
            P("rad", "ang", None),
            P("rad", "ang", None),
        ),
        out_specs=P(None, None, "ang", "rad", None),
        check_vma=False,
    )
```
